32 devices in a mesh: section: 2 (over core), dp: 4 (over y, x), mp: 4 (over z).
Axes of the slice: x: 2, y: 2, z: 4, core: 2. Of those that a mesh axis runs over, the one named last changes fastest.
Arguments:
- hidden_in: bfloat16 [2, 384, 8192], P('section', 'dp', 'mp'), may hold values from -6 to 6
- layer_gain: float32 [1, 2, 8192], P(None, 'section'), may hold values from 0.5 to 1.5
- gate_proj: bfloat16 [1, 2, 8192, 16384], P(None, 'section', 'dp', 'mp'), may hold values from -0.0625 to 0.0625
- up_proj: bfloat16 [1, 2, 8192, 16384], P(None, 'section', 'dp', 'mp'), may hold values from -0.0625 to 0.0625
- down_proj: bfloat16 [1, 2, 16384, 8192], P(None, 'section', 'mp', 'dp'), may hold values from -0.046875 to 0.046875
- final_gain: float32 [8192], P('mp'), may hold values from 0.5 to 1.5
- teacher_rows: bfloat16 [2, 4, 192, 8192], P('section', 'dp', None, 'mp'), may hold values from -6 to 6
- send_counts: int32 [2, 4, 4], P('section', 'dp'), may hold values from 0 to 48, as said below
- doc_ids: int32 [2, 4, 96], P('section', 'dp'), may hold values from 0 to 7, never falling along the last dimension, each value on 1 to 24 neighbouring positions
Outputs:
- d_hidden: float32 [2, 384, 8192], P('section', 'dp', 'mp')
- doc_loss: float32 [2, 4], P('section', 'dp')
The draws below stay inside these ranges and needn't reach their ends.
Inputs may be any that keep to these rules, and one draw needn't show every extreme that they name: For every micro-batch m and data group p the counts send_counts[m, q, p] over the 4 teacher shards q sum to exactly 96; in every such column some count equals 48. `doc_ids`: within each micro-batch of each data group the ids never fall, all 8 documents occur, each with 1 to 24 tokens, and one has exactly 24.
All inputs are finite; a program needn't handle non-finite values.
Results may differ from the reference program's by a relative error of at most 0.02.
Values may be sent and summed in bfloat16 or wider, within the bound.
No kernel may reach another device: no remote copies, remote signals or barrier semaphores. Data moves between devices by JAX's collectives and lax.ppermute only.
A program may use at most 320 MiB of HBM per device.

```python
import math
import jax
import jax.numpy as jnp
import numpy as np
from jax import lax

D = 8192
FF = 16384
REP = 1
DOCS = 8
TOK = 96
MICRO = 2
ROWS = 384
CAP = 48
DOC_MOST = 24
N_SECTION = 2
N_DP = 4
N_MP = 4


def draw_send_counts(key, part):
    half_cap = CAP // 2
    pair_count = N_DP // 2
    key_spread, key_pick, key_sign = jax.random.split(key, 3)
    spread = jax.random.randint(key_spread, (MICRO, pair_count, N_DP), -half_cap, half_cap + 1)
    chosen = jax.random.randint(key_pick, (MICRO, 1, N_DP), 0, pair_count)
    sign_flip = jax.random.randint(key_sign, (MICRO, 1, N_DP), 0, 2) * 2 - 1
    spread = jnp.where(jnp.arange(pair_count)[None, :, None] == chosen, half_cap * sign_flip, spread)
    stacked = jnp.stack([half_cap + spread, half_cap - spread], axis=2)
    return stacked.reshape(MICRO, N_DP, N_DP).astype(jnp.int32)


def block_levels(key, shape, pieces, least, high):
    factor_of = 1.0
    for position, parts in pieces:
        heights = jax.random.uniform(jax.random.fold_in(jax.random.fold_in(key, 6), position), (parts,), jnp.float32, least / len(pieces), high / len(pieces))
        factor_of = factor_of * jnp.repeat(jnp.exp(heights), shape[position] // parts).reshape((-1,) + (1,) * (len(shape) - 1 - position))
    return factor_of


def length_profile(count, total, most, lean):
    loads = [(1 << 20) // math.isqrt(standing ** lean) + 1 for standing in range(2, count + 1)]
    spare, given = total - most - (count - 1), [1] * (count - 1)
    while spare > 0:
        movable = [i for i in range(count - 1) if given[i] < most]
        whole, budget = sum([loads[i] for i in movable]), spare
        for i in movable:
            extra = min(most - given[i], max(1, budget * loads[i] // whole), spare)
            given[i] = given[i] + extra
            spare = spare - extra
    return np.array([most] + given)


def ragged_sizes(key, number_of, total, most, lean):
    if number_of == 2:
        one = jax.random.randint(key, (), max(1, total - most), min(most, total - 1) + 1)
        return jnp.stack([one, total - one])
    lengths = jnp.asarray(length_profile(number_of, total, most, lean), jnp.int32)
    pairs = (number_of - 1) // 2
    giver, taker = lengths[1:1 + 2 * pairs:2], lengths[2:2 + 2 * pairs:2]
    room = jnp.minimum(giver - 1, most - taker)
    passed = jax.random.randint(jax.random.fold_in(key, 1), (pairs,), 0, 1 << 20) % (room + 1)
    lengths = lengths.at[1:1 + 2 * pairs:2].set(giver - passed).at[2:2 + 2 * pairs:2].set(taker + passed)
    return lengths[jax.random.permutation(jax.random.fold_in(key, 2), number_of)]


def centred(own_key, shape, scale, most, shards=(), held_as=jnp.bfloat16):
    result = scale * jax.random.normal(own_key, shape, jnp.float32)
    if shards:
        result = result * block_levels(own_key, shape, shards, -0.22, 0.18)
    return jnp.clip(result, -most, most).astype(held_as)


def setup_inputs(seed: int = 0) -> dict:
    seeds = jax.random.split(jax.random.key(seed), 10)
    return {
        "hidden_in": centred(seeds[0], (MICRO, ROWS, D), 1.0, 6.0, ((0, 2), (1, 4), (2, 4))),
        "layer_gain": jnp.clip(1.0 + 0.1 * jax.random.normal(seeds[1], (REP, N_SECTION, D), jnp.float32), 0.5, 1.5),
        "gate_proj": centred(seeds[2], (REP, N_SECTION, D, FF), D ** -0.5, 0.0625, ((1, 2), (2, 4), (3, 4))),
        "up_proj": centred(seeds[3], (REP, N_SECTION, D, FF), D ** -0.5, 0.0625, ((1, 2), (2, 4), (3, 4))),
        "down_proj": centred(seeds[4], (REP, N_SECTION, FF, D), FF ** -0.5, 0.046875, ((1, 2), (2, 4), (3, 4))),
        "final_gain": jnp.clip(1.0 + 0.1 * jax.random.normal(seeds[5], (D,), jnp.float32), 0.5, 1.5),
        "teacher_rows": centred(seeds[6], (MICRO, N_DP, N_DP * CAP, D), 1.0, 6.0, ((0, 2), (1, 4), (3, 4))),
        "send_counts": draw_send_counts(jax.random.fold_in(seeds[9], 71), 0),
        "doc_ids": jax.vmap(lambda own: jnp.searchsorted(jnp.cumsum(ragged_sizes(own, DOCS, TOK, DOC_MOST, 1)), jnp.arange(TOK), side="right"))(jax.random.split(seeds[8], MICRO * N_DP)).reshape((MICRO, N_DP, TOK)).astype(jnp.int32),
    }


EPSILON = 1e-05

def feed_forward(carried, gain_row, gate_rows, up_rows, down_rows):
    wide_rows = carried.astype(jnp.float32)
    scale = lax.rsqrt(lax.optimization_barrier(jnp.mean(wide_rows * wide_rows, axis=-1, keepdims=True)) + EPSILON)
    normed = (wide_rows * scale * gain_row[None, :]).astype(jnp.bfloat16)
    gate_full = jnp.dot(normed, gate_rows, preferred_element_type=jnp.float32)
    up_full = jnp.dot(normed, up_rows, preferred_element_type=jnp.float32)
    inner = (jax.nn.silu(gate_full) * up_full).astype(jnp.bfloat16)
    block = FF // N_MP

    def add_block(index, total):
        start = (index * block).astype(jnp.int32)
        piece = lax.dynamic_slice_in_dim(inner, start, block, 1)
        weight_rows = lax.dynamic_slice_in_dim(down_rows, start, block, 0)
        term = jnp.dot(piece, weight_rows, preferred_element_type=jnp.float32).astype(jnp.bfloat16)
        term = lax.optimization_barrier(term)
        return total + term.astype(jnp.float32)
    summed = lax.fori_loop(0, N_MP, add_block, jnp.zeros(wide_rows.shape, jnp.float32))
    return (wide_rows + summed).astype(jnp.bfloat16)

def reference(hidden_in, layer_gain, gate_proj, up_proj, down_proj, final_gain, teacher_rows, send_counts, doc_ids):
    flat_rows = hidden_in.reshape(-1, D)
    for repeat_pos in range(REP):
        for phase_pos in range(N_SECTION):
            flat_rows = feed_forward(flat_rows, layer_gain[repeat_pos, phase_pos], gate_proj[repeat_pos, phase_pos], up_proj[repeat_pos, phase_pos], down_proj[repeat_pos, phase_pos])
    final_rows = flat_rows.reshape(MICRO, N_DP, TOK, D).astype(jnp.float32)
    columns = jnp.transpose(send_counts, (0, 2, 1)).astype(jnp.int32)
    end_rows = jnp.cumsum(columns, axis=-1).astype(jnp.int32)
    starts = (end_rows - columns).astype(jnp.int32)
    positions = jnp.arange(TOK, dtype=jnp.int32)
    source_of = lax.optimization_barrier(jnp.sum((end_rows[:, :, None, :] <= positions[None, None, :, None]).astype(jnp.int32), axis=-1)).astype(jnp.int32)
    first_row = jnp.take_along_axis(starts, source_of, axis=-1).astype(jnp.int32)
    slot_col = (jnp.arange(N_DP, dtype=jnp.int32)[None, :, None] * CAP + positions[None, None, :] - first_row).astype(jnp.int32)
    micro_index = jnp.arange(MICRO, dtype=jnp.int32)[:, None, None]
    targets = teacher_rows[micro_index, source_of, slot_col].astype(jnp.float32)
    member = (doc_ids[..., None] == jnp.arange(DOCS, dtype=jnp.int32)[None, None, None, :]).astype(jnp.float32)
    doc_sizes = lax.optimization_barrier(jnp.sum(member, axis=2))
    row_weight = lax.optimization_barrier(jnp.sum(member * (1.0 / doc_sizes)[:, :, None, :], axis=-1))
    rscale = lax.rsqrt(lax.optimization_barrier(jnp.mean(final_rows * final_rows, axis=-1, keepdims=True)) + EPSILON)
    normal_rows = final_rows * rscale
    student = normal_rows * final_gain
    residual = student - targets
    d_student = row_weight[..., None] * residual
    inner_sum = lax.optimization_barrier(jnp.sum(normal_rows * final_gain * d_student, axis=-1, keepdims=True))
    d_hidden = rscale * (final_gain * d_student - normal_rows * inner_sum / D)
    errors = lax.optimization_barrier(jnp.sum(residual * residual, axis=-1))
    doc_loss = lax.optimization_barrier(jnp.sum(row_weight * 0.5 * errors, axis=-1)) / (DOCS * D)
    return (d_hidden.reshape(MICRO, N_DP * TOK, D), doc_loss)
```

```python
import functools

import jax
import jax.numpy as jnp
from jax import lax
from jax.experimental import pallas as pl
from jax.experimental.pallas import tpu as pltpu
from jax.sharding import PartitionSpec as P

D = 8192
DOCS = 8
EPSILON = 1e-05
AXES = ("section", "dp", "mp")
TILE = 512
HALVES = 2
VMEM_LIMIT = 40 * 1024 * 1024


def swap_section(value):
    return lax.ppermute(value, "section", [(0, 1), (1, 0)])


def transpose_mesh(value):
    pairs = [(d * 4 + m, m * 4 + d) for d in range(4) for m in range(4)]
    return lax.ppermute(value, ("dp", "mp"), pairs)


def swap_dp(value, e):
    return lax.ppermute(value, "dp", [(d, d ^ e) for d in range(4)])


def swap_mp(value, k):
    return lax.ppermute(value, "mp", [(m, m ^ k) for m in range(4)])


def exchange(value, axis):
    return lax.all_to_all(value, axis, split_axis=0, concat_axis=0, tiled=True)


def either(is_own, start_own, start_other):
    pl.when(is_own)(start_own)
    pl.when(jnp.logical_not(is_own))(start_other)


def gate_up_kernel(number, first, swapped, x0, x1, x2, x3, gain_ref, gate0, up0, gate1, up1, keep_ref, send_ref, rows_ref, held, sems):
    step = pl.program_id(0)
    steps = pl.num_programs(0)
    is_own = lax.axis_index("section") == number
    own_place = lax.axis_index("dp") ^ lax.axis_index("mp")
    count = x0.shape[0]

    def fetch(j, tile):
        slot = 2 * lax.rem(tile, 2) + j
        columns = pl.ds(pl.multiple_of(first + tile * TILE, TILE), TILE)

        def copy(source):
            return lambda: pltpu.make_async_copy(source.at[:, columns], held.at[slot], sems.at[slot]).start()

        either(is_own, copy((gate0, up0)[j]), copy((gate1, up1)[j]))

    @pl.when(step == 0)
    def _():
        fetch(0, 0)
        fetch(1, 0)
        for k, ref in enumerate((x0, x1, x2, x3)):
            place = own_place ^ k
            if swapped:
                place = 2 * (place % 2) + place // 2
            piece = ref[...].astype(jnp.float32) * gain_ref[...]
            rows_ref[pl.ds(pl.multiple_of(place * count, count), count), :] = piece.astype(jnp.bfloat16)

    for j in range(2):

        @pl.when(step + 1 < steps)
        def _():
            fetch(j, step + 1)

        slot = 2 * lax.rem(step, 2) + j
        pltpu.make_async_copy(gate0.at[:, pl.ds(0, TILE)], held.at[slot], sems.at[slot]).wait()
        product = jnp.dot(rows_ref[...], held[slot], preferred_element_type=jnp.float32)
        keep_ref[j] = product[: 2 * count]
        send_ref[j] = product[2 * count :].astype(jnp.bfloat16)


def gate_up(number, first, width, swapped, rows, gain_row, own, received):
    groups = 4
    count, depth = rows[0].shape
    whole = lambda shape: pl.BlockSpec(shape, lambda t: (0,) * len(shape))
    return pl.pallas_call(
        functools.partial(gate_up_kernel, number, first, swapped),
        grid=(width // TILE,),
        in_specs=[whole((count, depth))] * 4 + [whole((1, depth))] + [pl.BlockSpec(memory_space=pl.ANY)] * 4,
        out_specs=[pl.BlockSpec((2, 2 * count, TILE), lambda t: (0, 0, t))] * 2,
        out_shape=[
            jax.ShapeDtypeStruct((2, 2 * count, width), jnp.float32),
            jax.ShapeDtypeStruct((2, 2 * count, width), jnp.bfloat16),
        ],
        scratch_shapes=[
            pltpu.VMEM((groups * count, depth), jnp.bfloat16),
            pltpu.VMEM((4, depth, TILE), jnp.bfloat16),
            pltpu.SemaphoreType.DMA((4,)),
        ],
        compiler_params=pltpu.CompilerParams(vmem_limit_bytes=VMEM_LIMIT),
        cost_estimate=pl.CostEstimate(
            flops=4 * groups * count * depth * width, bytes_accessed=4 * depth * width, transcendentals=0
        ),
        name="gate_up",
    )(*rows, gain_row, *own, *received)


def down_kernel(number, x0, x1, x2, x3a, x3b, own, received, out_ref, rows_ref, held, sems):
    step = pl.program_id(0)
    steps = pl.num_programs(0)
    is_own = lax.axis_index("section") == number
    data_pos = lax.axis_index("dp")
    groups = 4
    count, depth = x0.shape

    def fetch(tile):
        slot = lax.rem(tile, 2)
        columns = pl.ds(pl.multiple_of(tile * TILE, TILE), TILE)

        def copy(source):
            return lambda: pltpu.make_async_copy(source.at[:, columns], held.at[slot], sems.at[slot]).start()

        either(is_own, copy(own), copy(received))

    @pl.when(step == 0)
    def _():
        fetch(0)
        for e, piece in enumerate((x0, x1, x2)):
            rows_ref[pl.ds(pl.multiple_of((data_pos ^ e) * count, count), count), :] = piece[...]
        corner = pl.ds(pl.multiple_of((data_pos ^ 3) * count, count), count)
        rows_ref[corner, : depth // 2] = x3a[...]
        rows_ref[corner, depth // 2 :] = x3b[...]

    @pl.when(step + 1 < steps)
    def _():
        fetch(step + 1)

    slot = lax.rem(step, 2)
    pltpu.make_async_copy(own.at[:, pl.ds(0, TILE)], held.at[slot], sems.at[slot]).wait()
    product = jnp.dot(rows_ref[...], held[slot], preferred_element_type=jnp.float32)
    for g in range(groups):
        out_ref[g] = product[g * count : (g + 1) * count].astype(jnp.bfloat16)


def down_terms(number, pieces, own, received):
    groups = 4
    count, depth = pieces[0].shape
    features = own.shape[1]
    return pl.pallas_call(
        functools.partial(down_kernel, number),
        grid=(features // TILE,),
        in_specs=[pl.BlockSpec(piece.shape, lambda t: (0, 0)) for piece in pieces]
        + [pl.BlockSpec(memory_space=pl.ANY)] * 2,
        out_specs=pl.BlockSpec((groups, count, TILE), lambda t: (0, 0, t)),
        out_shape=jax.ShapeDtypeStruct((groups, count, features), jnp.bfloat16),
        scratch_shapes=[
            pltpu.VMEM((groups * count, depth), jnp.bfloat16),
            pltpu.VMEM((2, depth, TILE), jnp.bfloat16),
            pltpu.SemaphoreType.DMA((2,)),
        ],
        compiler_params=pltpu.CompilerParams(vmem_limit_bytes=VMEM_LIMIT),
        cost_estimate=pl.CostEstimate(
            flops=2 * groups * count * depth * features, bytes_accessed=2 * depth * features, transcendentals=0
        ),
        name="down",
    )(*pieces, own, received)


def sum_squares(rows):
    squares = jnp.stack([jnp.sum(jnp.square(piece.astype(jnp.float32)), axis=-1) for piece in rows])
    own_place = lax.axis_index("dp") ^ lax.axis_index("mp")
    keep, send = [jnp.stack([squares[i ^ own_place] for i in pair]) for pair in ((0, 2), (1, 3))]
    keep = keep + swap_dp(send, 1)
    return keep[0] + swap_dp(keep[1], 2)


def stream(number, first, width, steps, rows, gain_row, own, received):
    keep, send = gate_up(number, first, width, steps[0] == 1, rows, gain_row, own, received)
    count = rows[0].shape[0]
    got = swap_dp(send, steps[0])
    onward = (keep[:, count:] + got[:, count:].astype(jnp.float32)).astype(jnp.bfloat16)
    last = swap_dp(onward, steps[1])
    return keep[:, :count] + got[:, :count].astype(jnp.float32) + last.astype(jnp.float32)


def enter(own):
    return [own] + [swap_mp(own, k) for k in (1, 2, 3)]


def layer(number, own, rows, gain_row, weights, received):
    half = weights[0].shape[1] // 2
    scale = lax.rsqrt(sum_squares(rows) / D + EPSILON)[:, None]
    args = (rows, gain_row, weights[:2], received[:2])
    inner = []
    for total in (stream(number, 0, half, (1, 2), *args), stream(number, half, half, (2, 1), *args)):
        inner.append((jax.nn.silu(total[0] * scale) * (total[1] * scale)).astype(jnp.bfloat16))
    inner = jnp.concatenate(inner, axis=1)
    along_x = swap_dp(inner, 1)
    along_y = swap_dp(inner, 2)
    corner = (swap_dp(along_y[:, :half], 1), swap_dp(along_x[:, half:], 2))
    terms = down_terms(number, (inner, along_x, along_y) + corner, weights[2], received[2])
    terms = exchange(terms, "mp")
    return (own.astype(jnp.float32) + jnp.sum(terms.astype(jnp.float32), axis=0)).astype(jnp.bfloat16)


def fast_final(hidden_in, layer_gain, gate, up, down, targets):
    tokens, features = hidden_in.shape[1:]
    count = tokens // HALVES
    is_first = lax.axis_index("section") == 0
    gain = lax.dynamic_slice_in_dim(layer_gain[0, 0], lax.axis_index("dp") * features, features, 0)
    other_gain = swap_section(gain)
    owns = [transpose_mesh(hidden_in[0, i * count : (i + 1) * count]) for i in range(HALVES)]
    other_gate, other_up = swap_section(gate), swap_section(up)
    rows = [enter(owns[0])]
    rows[0], targets, later_down = lax.optimization_barrier((rows[0], targets, down))
    received = (other_gate, other_up, swap_section(later_down))
    rows += [enter(own) for own in owns[1:]]
    for number in range(2):
        gain_row = jnp.where(is_first == (number == 0), gain, other_gain)[None, :]
        if number:
            rows = [enter(own) for own in owns]
        owns = [layer(number, own, piece, gain_row, (gate, up, down), received) for own, piece in zip(owns, rows)]
    return jnp.concatenate([transpose_mesh(own) for own in owns], axis=0), targets


def fast_targets(teacher, counts, token_count):
    capacity = teacher.shape[0] // 4
    features = teacher.shape[1]
    arrived = lax.all_to_all(
        teacher.reshape(4, capacity, features), "dp", split_axis=0, concat_axis=0, tiled=True
    )
    all_counts = lax.all_to_all(
        counts.reshape(4, 1).astype(jnp.bfloat16), "dp", split_axis=0, concat_axis=0, tiled=True
    )
    per_source = all_counts[:, 0].astype(jnp.int32)
    end_rows = jnp.cumsum(per_source)
    starts = end_rows - per_source
    positions = jnp.arange(token_count, dtype=jnp.int32)
    source_of = jnp.sum((end_rows[None, :] <= positions[:, None]).astype(jnp.int32), axis=1)
    matching = source_of[:, None] == jnp.arange(4, dtype=jnp.int32)[None, :]
    first_row = jnp.sum(jnp.where(matching, starts[None, :], 0), axis=1)
    flat_index = source_of * capacity + positions - first_row
    return arrived.reshape(-1, features)[flat_index].astype(jnp.float32)


def weights_of_rows(doc_row):
    member = (doc_row[:, None] == jnp.arange(DOCS, dtype=jnp.int32)[None, :]).astype(jnp.float32)
    doc_sizes = jnp.sum(member, axis=0)
    return jnp.sum(member * (1.0 / doc_sizes)[None, :], axis=1)


def distil(final, targets, row_weight, final_gain, sum_features):
    wide = final.astype(jnp.float32)
    gain_row = final_gain[None, :]
    squares = sum_features(jnp.sum(wide * wide, axis=-1))
    rscale = lax.rsqrt(squares / D + EPSILON)
    normal_rows = wide * rscale[:, None]
    residual = normal_rows * gain_row - targets
    d_student = row_weight[:, None] * residual
    sums = sum_features(
        jnp.stack(
            [
                jnp.sum(normal_rows * gain_row * d_student, axis=-1),
                jnp.sum(residual * residual, axis=-1),
            ]
        )
    )
    d_hidden = rscale[:, None] * (gain_row * d_student - normal_rows * sums[0][:, None] / D)
    doc_loss = jnp.sum(row_weight * 0.5 * sums[1]) / (DOCS * D)
    return d_hidden[None], doc_loss.reshape(1, 1)


def distil_once(final, targets, row_weight, final_gain):
    wide = final.astype(jnp.float32)
    features = wide.shape[1]
    gained = wide * final_gain[None, :]
    squares = jnp.sum(wide * wide, axis=-1)
    rough = gained * lax.rsqrt(squares / features + EPSILON)[:, None] - targets
    local = jnp.stack(
        [squares, jnp.sum(rough * rough, axis=-1), jnp.sum(gained * rough, axis=-1), jnp.sum(gained * gained, axis=-1)]
    )
    squares, rough_squares, crossed, gained_squares = jnp.moveaxis(lax.all_gather(local, "mp"), 1, 0)
    rscale = lax.rsqrt(jnp.sum(squares, axis=0) / D + EPSILON)
    shift = rscale[None, :] - lax.rsqrt(squares / features + EPSILON)
    errors = jnp.sum(rough_squares + shift * (2.0 * crossed + shift * gained_squares), axis=0)
    inner_sum = row_weight * rscale * jnp.sum(crossed + shift * gained_squares, axis=0)
    gain_row = final_gain[None, :]
    normal_rows = wide * rscale[:, None]
    d_student = row_weight[:, None] * (normal_rows * gain_row - targets)
    d_hidden = rscale[:, None] * (gain_row * d_student - normal_rows * inner_sum[:, None] / D)
    doc_loss = jnp.sum(row_weight * 0.5 * errors) / (DOCS * D)
    return d_hidden[None], doc_loss.reshape(1, 1)


def fast_body(
    hidden_in, layer_gain, gate_proj, up_proj, down_proj, final_gain, teacher_rows, send_counts, doc_ids
):
    targets = fast_targets(teacher_rows[0, 0], send_counts[0, 0], hidden_in.shape[1])
    final, targets = fast_final(
        hidden_in, layer_gain, gate_proj[0, 0], up_proj[0, 0], down_proj[0, 0], targets
    )
    return distil_once(final, targets, weights_of_rows(doc_ids[0, 0]), final_gain)


def wide_layer(rows, gain_row, gate, up, down):
    wide = rows.astype(jnp.float32)
    squares = lax.psum(jnp.sum(wide * wide, axis=-1, keepdims=True), "dp")
    scale = lax.rsqrt(squares / D + EPSILON)
    normed = (wide * scale * gain_row[None, :]).astype(jnp.bfloat16)
    both = jnp.stack(
        [jnp.dot(normed, weight, preferred_element_type=jnp.float32) for weight in (gate, up)]
    )
    total = lax.psum_scatter(both, "dp", scatter_dimension=1, tiled=True)
    inner = (jax.nn.silu(total[0]) * total[1]).astype(jnp.bfloat16)
    inner = lax.all_gather(inner, "dp", axis=0, tiled=True)
    term = jnp.dot(inner, down, preferred_element_type=jnp.float32)
    return (wide + lax.psum(term, "mp")).astype(jnp.bfloat16)


def wide_body(
    hidden_in, layer_gain, gate_proj, up_proj, down_proj, final_gain, teacher_rows, send_counts, doc_ids
):
    phases = lax.axis_size("section")
    count_data = lax.axis_size("dp")
    phase_pos = lax.axis_index("section")
    data_pos = lax.axis_index("dp")
    model_pos = lax.axis_index("mp")
    tokens, narrow = hidden_in.shape[1:]
    rows = lax.all_gather(hidden_in[0], "section", axis=0)
    rows = lax.all_gather(rows, "mp", axis=2, tiled=True)
    rows = lax.all_to_all(rows, "dp", split_axis=2, concat_axis=1, tiled=True)
    features = rows.shape[2]
    rows = rows.reshape(-1, features)
    ring = [(s, (s + 1) % phases) for s in range(phases)]
    for repeat in range(gate_proj.shape[0]):
        gain_row = lax.dynamic_slice_in_dim(layer_gain[repeat, 0], data_pos * features, features, 0)
        for phase in range(phases):
            fresh = wide_layer(
                rows, gain_row, gate_proj[repeat, 0], up_proj[repeat, 0], down_proj[repeat, 0]
            )
            rows = lax.ppermute(jnp.where(phase_pos == phase, fresh, rows), "section", ring)
    rows = lax.all_gather(rows, "section", axis=0)[0]
    rows = lax.dynamic_index_in_dim(
        rows.reshape(phases, count_data * tokens, features), phase_pos, 0, keepdims=False
    )
    rows = lax.all_to_all(rows, "dp", split_axis=0, concat_axis=1, tiled=True)
    final = lax.dynamic_slice_in_dim(rows, model_pos * narrow, narrow, 1)
    teacher = teacher_rows[0, 0].reshape(count_data, -1, narrow)
    capacity = teacher.shape[1]
    arrived = lax.all_to_all(teacher, "dp", split_axis=0, concat_axis=0, tiled=True)
    counts = lax.all_gather(send_counts[0, 0], "dp", axis=0)
    per_source = lax.dynamic_index_in_dim(counts, data_pos, 1, keepdims=False)
    end_rows = jnp.cumsum(per_source)
    starts = end_rows - per_source
    positions = jnp.arange(tokens, dtype=jnp.int32)
    source_of = jnp.sum((end_rows[None, :] <= positions[:, None]).astype(jnp.int32), axis=1)
    flat_index = source_of * capacity + positions - starts[source_of]
    targets = arrived.reshape(-1, narrow)[flat_index].astype(jnp.float32)
    return distil(
        final,
        targets,
        weights_of_rows(doc_ids[0, 0]),
        final_gain,
        lambda value: lax.psum(value, "mp"),
    )


def solution(mesh):
    in_specs = (
        P("section", "dp", "mp"),
        P(None, "section", None),
        P(None, "section", "dp", "mp"),
        P(None, "section", "dp", "mp"),
        P(None, "section", "mp", "dp"),
        P("mp"),
        P("section", "dp", None, "mp"),
        P("section", "dp", None),
        P("section", "dp", None),
    )
    out_specs = (P("section", "dp", "mp"), P("section", "dp"))
    sizes = tuple(mesh.shape[axis] for axis in AXES)
    body = fast_body if sizes == (2, 4, 4) else wide_body
    return jax.shard_map(body, mesh=mesh, in_specs=in_specs, out_specs=out_specs, check_vma=False)
```

```python
import functools

import jax
import jax.numpy as jnp
from jax import lax
from jax.experimental import pallas as pl
from jax.experimental.pallas import tpu as pltpu
from jax.sharding import PartitionSpec as P

D = 8192
DOCS = 8
EPSILON = 1e-05
AXES = ("section", "dp", "mp")
TILE = 512
COST = 1
VMEM_LIMIT = 40 * 1024 * 1024


def swap_section(value):
    return lax.ppermute(value, "section", [(0, 1), (1, 0)])


def transpose_mesh(value):
    pairs = [(d * 4 + m, m * 4 + d) for d in range(4) for m in range(4)]
    return lax.ppermute(value, ("dp", "mp"), pairs)


def swap_dp(value, e):
    return lax.ppermute(value, "dp", [(d, d ^ e) for d in range(4)])


def swap_mp(value, k):
    return lax.ppermute(value, "mp", [(m, m ^ k) for m in range(4)])


def exchange(value, axis):
    return lax.all_to_all(value, axis, split_axis=0, concat_axis=0, tiled=True)


def either(is_own, start_own, start_other):
    pl.when(is_own)(start_own)
    pl.when(jnp.logical_not(is_own))(start_other)


def gate_up_kernel(number, first, swapped, relative, x0, x1, x2, x3, gain_ref, gate0, up0, gate1, up1, keep_ref, send_ref, rows_ref, held, sems):
    step = pl.program_id(0)
    steps = pl.num_programs(0)
    is_own = lax.axis_index("section") == number
    own_place = lax.axis_index("dp")
    if relative:
        own_place = own_place ^ lax.axis_index("mp")
    count = x0.shape[0]

    def fetch(j, tile):
        slot = 2 * lax.rem(tile, 2) + j
        columns = pl.ds(pl.multiple_of(first + tile * TILE, TILE), TILE)

        def copy(source):
            return lambda: pltpu.make_async_copy(source.at[:, columns], held.at[slot], sems.at[slot]).start()

        either(is_own, copy((gate0, up0)[j]), copy((gate1, up1)[j]))

    @pl.when(step == 0)
    def _():
        fetch(0, 0)
        fetch(1, 0)
        for k, ref in enumerate((x0, x1, x2, x3)):
            place = own_place ^ k
            if swapped:
                place = 2 * (place % 2) + place // 2
            piece = ref[...].astype(jnp.float32) * gain_ref[...]
            rows_ref[pl.ds(pl.multiple_of(place * count, count), count), :] = piece.astype(jnp.bfloat16)

    for j in range(2):

        @pl.when(step + 1 < steps)
        def _():
            fetch(j, step + 1)

        slot = 2 * lax.rem(step, 2) + j
        pltpu.make_async_copy(gate0.at[:, pl.ds(0, TILE)], held.at[slot], sems.at[slot]).wait()
        product = jnp.dot(rows_ref[...], held[slot], preferred_element_type=jnp.float32)
        keep_ref[j] = product[: 2 * count]
        send_ref[j] = product[2 * count :].astype(jnp.bfloat16)


def gate_up(number, first, width, swapped, rows, gain_row, own, received):
    groups = 4
    relative = isinstance(rows, list)
    count, depth = rows[0].shape
    whole = lambda shape: pl.BlockSpec(shape, lambda t: (0,) * len(shape))
    if relative:
        piece_specs = [whole((count, depth))] * 4
    else:
        piece_specs = [pl.BlockSpec((None, count, depth), lambda t, k=k: (k, 0, 0)) for k in range(4)]
        rows = [rows] * 4
    return pl.pallas_call(
        functools.partial(gate_up_kernel, number, first, swapped, relative),
        grid=(width // TILE,),
        in_specs=piece_specs + [whole((1, depth))] + [pl.BlockSpec(memory_space=pl.ANY)] * 4,
        out_specs=[pl.BlockSpec((2, 2 * count, TILE), lambda t: (0, 0, t))] * 2,
        out_shape=[
            jax.ShapeDtypeStruct((2, 2 * count, width), jnp.float32),
            jax.ShapeDtypeStruct((2, 2 * count, width), jnp.bfloat16),
        ],
        scratch_shapes=[
            pltpu.VMEM((groups * count, depth), jnp.bfloat16),
            pltpu.VMEM((4, depth, TILE), jnp.bfloat16),
            pltpu.SemaphoreType.DMA((4,)),
        ],
        compiler_params=pltpu.CompilerParams(vmem_limit_bytes=VMEM_LIMIT),
        cost_estimate=pl.CostEstimate(
            flops=4 * groups * count * depth * width // COST,
            bytes_accessed=4 * depth * width // COST,
            transcendentals=0,
        ),
        name="gate_up",
    )(*rows, gain_row, *own, *received)


def down_kernel(number, x0, x1, x2, x3a, x3b, own, received, out_ref, rows_ref, held, sems):
    step = pl.program_id(0)
    steps = pl.num_programs(0)
    is_own = lax.axis_index("section") == number
    data_pos = lax.axis_index("dp")
    groups = 4
    count, depth = x0.shape

    def fetch(tile):
        slot = lax.rem(tile, 2)
        columns = pl.ds(pl.multiple_of(tile * TILE, TILE), TILE)

        def copy(source):
            return lambda: pltpu.make_async_copy(source.at[:, columns], held.at[slot], sems.at[slot]).start()

        either(is_own, copy(own), copy(received))

    @pl.when(step == 0)
    def _():
        fetch(0)
        for e, piece in enumerate((x0, x1, x2)):
            rows_ref[pl.ds(pl.multiple_of((data_pos ^ e) * count, count), count), :] = piece[...]
        corner = pl.ds(pl.multiple_of((data_pos ^ 3) * count, count), count)
        rows_ref[corner, : depth // 2] = x3a[...]
        rows_ref[corner, depth // 2 :] = x3b[...]

    @pl.when(step + 1 < steps)
    def _():
        fetch(step + 1)

    slot = lax.rem(step, 2)
    pltpu.make_async_copy(own.at[:, pl.ds(0, TILE)], held.at[slot], sems.at[slot]).wait()
    product = jnp.dot(rows_ref[...], held[slot], preferred_element_type=jnp.float32)
    for g in range(groups):
        out_ref[g] = product[g * count : (g + 1) * count].astype(jnp.bfloat16)


def down_terms(number, pieces, own, received):
    groups = 4
    count, depth = pieces[0].shape
    features = own.shape[1]
    return pl.pallas_call(
        functools.partial(down_kernel, number),
        grid=(features // TILE,),
        in_specs=[pl.BlockSpec(piece.shape, lambda t: (0, 0)) for piece in pieces]
        + [pl.BlockSpec(memory_space=pl.ANY)] * 2,
        out_specs=pl.BlockSpec((groups, count, TILE), lambda t: (0, 0, t)),
        out_shape=jax.ShapeDtypeStruct((groups, count, features), jnp.bfloat16),
        scratch_shapes=[
            pltpu.VMEM((groups * count, depth), jnp.bfloat16),
            pltpu.VMEM((2, depth, TILE), jnp.bfloat16),
            pltpu.SemaphoreType.DMA((2,)),
        ],
        compiler_params=pltpu.CompilerParams(vmem_limit_bytes=VMEM_LIMIT),
        cost_estimate=pl.CostEstimate(
            flops=2 * groups * count * depth * features // COST,
            bytes_accessed=2 * depth * features // COST,
            transcendentals=0,
        ),
        name="down",
    )(*pieces, own, received)


def squares_by_place(rows):
    squares = jnp.stack([jnp.sum(jnp.square(rows[k].astype(jnp.float32)), axis=-1) for k in range(4)])
    own_place = lax.axis_index("dp")
    if isinstance(rows, list):
        own_place = own_place ^ lax.axis_index("mp")
    return [squares[i ^ own_place] for i in range(4)]


def tie(value, *earlier):
    return lax.optimization_barrier((value, earlier))[0]


def sum_squares(chunks, late):
    places = [jnp.stack(pieces) for pieces in zip(*[squares_by_place(rows) for rows in chunks])]
    keep, send = jnp.stack(places[0::2]), jnp.stack(places[1::2])
    got = swap_dp(send, 1)
    keep = keep + tie(got, late)
    return keep[0] + swap_dp(keep[1], 2)


def sum_first(partial, step):
    keep, send = partial
    count = keep.shape[1] // 2
    got = swap_dp(send, step)
    onward = (keep[:, count:] + got[:, count:].astype(jnp.float32)).astype(jnp.bfloat16)
    return keep[:, :count], got[:, :count], onward


def sum_second(state, step):
    keep, got, onward = state
    return keep + got.astype(jnp.float32) + swap_dp(onward, step).astype(jnp.float32)


def enter(own):
    return [own] + [swap_mp(own, k) for k in (1, 2, 3)]


def add_terms(own, terms):
    return (own.astype(jnp.float32) + jnp.sum(terms.astype(jnp.float32), axis=0)).astype(jnp.bfloat16)


def activate(states, squares):
    scale = lax.rsqrt(squares / D + EPSILON)[:, None]
    inner = []
    for state, step in zip(states, (2, 1)):
        total = sum_second(state, step) * scale
        inner.append((jax.nn.silu(total[0]) * total[1]).astype(jnp.bfloat16))
    return jnp.concatenate(inner, axis=1)


def fast_final(hidden_in, layer_gain, gate, up, down, teacher, counts):
    tokens, features = hidden_in.shape[1:]
    half = gate.shape[1] // 2
    count = tokens // 2
    is_first = lax.axis_index("section") == 0
    gain = lax.dynamic_slice_in_dim(layer_gain[0, 0], lax.axis_index("dp") * features, features, 0)
    other_gain = swap_section(gain)
    early_gate, early_up = tie((gate, up), other_gain)
    received = [swap_section(early_gate), swap_section(early_up)]
    owns = [transpose_mesh(hidden_in[0, i * count : (i + 1) * count]) for i in range(2)]
    targets = fast_targets(*tie((teacher, counts), owns[0]), tokens)
    for number in range(2):
        gain_row = jnp.where(is_first == (number == 0), gain, other_gain)[None, :]

        def products(which, pieces):
            return gate_up(
                number, which * half, half, which == 0, pieces, gain_row, (gate, up), received[:2]
            )

        if not number:
            rows = enter(owns[0])
            rows, owns[1], targets, later_down = lax.optimization_barrier((rows, owns[1], targets, down))
            received.append(swap_section(later_down))
            later_rows = enter(owns[1])
        first, second = products(0, rows), products(1, rows)
        later_rows = tie(later_rows, second[0])
        states = [sum_first(first, 1), sum_first(second, 2)]
        later_first = products(0, later_rows)
        later_second = products(1, tie(later_rows, states[0][2]))
        later_states = [sum_first(later_first, 1), sum_first(later_second, 2)]
        squares, later_squares = sum_squares([rows, later_rows], later_second[0])
        inner, later_inner = activate(states, squares), activate(later_states, later_squares)
        along = [swap_dp(inner, 1), swap_dp(inner, 2)]
        later_along = [swap_dp(later_inner, 1), swap_dp(later_inner, 2)]
        corner = [swap_dp(along[1][:, :half], 1), swap_dp(along[0][:, half:], 2)]
        terms = exchange(down_terms(number, [inner] + along + corner, down, received[2]), "mp")
        corner = [swap_dp(later_along[1][:, :half], 1), swap_dp(later_along[0][:, half:], 2)]
        owns[0] = add_terms(owns[0], terms)
        if not number:
            rows = enter(owns[0])
        terms = down_terms(number, [later_inner] + later_along + corner, down, received[2])
        rows = tie(rows, terms)
        owns[1] = add_terms(owns[1], exchange(tie(terms, owns[0]), "mp"))
        if not number:
            later_rows = enter(owns[1])
    return jnp.concatenate([transpose_mesh(own) for own in owns], axis=0), targets


def fast_targets(teacher, counts, token_count):
    capacity = teacher.shape[0] // 4
    features = teacher.shape[1]
    arrived = lax.all_to_all(
        teacher.reshape(4, capacity, features), "dp", split_axis=0, concat_axis=0, tiled=True
    )
    all_counts = lax.all_to_all(
        counts.reshape(4, 1).astype(jnp.bfloat16), "dp", split_axis=0, concat_axis=0, tiled=True
    )
    per_source = all_counts[:, 0].astype(jnp.int32)
    end_rows = jnp.cumsum(per_source)
    starts = end_rows - per_source
    positions = jnp.arange(token_count, dtype=jnp.int32)
    source_of = jnp.sum((end_rows[None, :] <= positions[:, None]).astype(jnp.int32), axis=1)
    matching = source_of[:, None] == jnp.arange(4, dtype=jnp.int32)[None, :]
    first_row = jnp.sum(jnp.where(matching, starts[None, :], 0), axis=1)
    flat_index = source_of * capacity + positions - first_row
    return arrived.reshape(-1, features)[flat_index].astype(jnp.float32)


def weights_of_rows(doc_row):
    member = (doc_row[:, None] == jnp.arange(DOCS, dtype=jnp.int32)[None, :]).astype(jnp.float32)
    doc_sizes = jnp.sum(member, axis=0)
    return jnp.sum(member * (1.0 / doc_sizes)[None, :], axis=1)


def distil(final, targets, row_weight, final_gain, sum_features):
    wide = final.astype(jnp.float32)
    gain_row = final_gain[None, :]
    squares = sum_features(jnp.sum(wide * wide, axis=-1))
    rscale = lax.rsqrt(squares / D + EPSILON)
    normal_rows = wide * rscale[:, None]
    residual = normal_rows * gain_row - targets
    d_student = row_weight[:, None] * residual
    sums = sum_features(
        jnp.stack(
            [
                jnp.sum(normal_rows * gain_row * d_student, axis=-1),
                jnp.sum(residual * residual, axis=-1),
            ]
        )
    )
    d_hidden = rscale[:, None] * (gain_row * d_student - normal_rows * sums[0][:, None] / D)
    doc_loss = jnp.sum(row_weight * 0.5 * sums[1]) / (DOCS * D)
    return d_hidden[None], doc_loss.reshape(1, 1)


def distil_once(final, targets, row_weight, final_gain):
    wide = final.astype(jnp.float32)
    features = wide.shape[1]
    gained = wide * final_gain[None, :]
    squares = jnp.sum(wide * wide, axis=-1)
    rough = gained * lax.rsqrt(squares / features + EPSILON)[:, None] - targets
    local = jnp.stack(
        [squares, jnp.sum(rough * rough, axis=-1), jnp.sum(gained * rough, axis=-1), jnp.sum(gained * gained, axis=-1)]
    )
    squares, rough_squares, crossed, gained_squares = jnp.moveaxis(lax.all_gather(local, "mp"), 1, 0)
    rscale = lax.rsqrt(jnp.sum(squares, axis=0) / D + EPSILON)
    shift = rscale[None, :] - lax.rsqrt(squares / features + EPSILON)
    errors = jnp.sum(rough_squares + shift * (2.0 * crossed + shift * gained_squares), axis=0)
    inner_sum = row_weight * rscale * jnp.sum(crossed + shift * gained_squares, axis=0)
    gain_row = final_gain[None, :]
    normal_rows = wide * rscale[:, None]
    d_student = row_weight[:, None] * (normal_rows * gain_row - targets)
    d_hidden = rscale[:, None] * (gain_row * d_student - normal_rows * inner_sum[:, None] / D)
    doc_loss = jnp.sum(row_weight * 0.5 * errors) / (DOCS * D)
    return d_hidden[None], doc_loss.reshape(1, 1)


def fast_body(
    hidden_in, layer_gain, gate_proj, up_proj, down_proj, final_gain, teacher_rows, send_counts, doc_ids
):
    final, targets = fast_final(
        hidden_in,
        layer_gain,
        gate_proj[0, 0],
        up_proj[0, 0],
        down_proj[0, 0],
        teacher_rows[0, 0],
        send_counts[0, 0],
    )
    return distil_once(final, targets, weights_of_rows(doc_ids[0, 0]), final_gain)


def wide_layer(rows, gain_row, gate, up, down):
    wide = rows.astype(jnp.float32)
    squares = lax.psum(jnp.sum(wide * wide, axis=-1, keepdims=True), "dp")
    scale = lax.rsqrt(squares / D + EPSILON)
    normed = (wide * scale * gain_row[None, :]).astype(jnp.bfloat16)
    both = jnp.stack(
        [jnp.dot(normed, weight, preferred_element_type=jnp.float32) for weight in (gate, up)]
    )
    total = lax.psum_scatter(both, "dp", scatter_dimension=1, tiled=True)
    inner = (jax.nn.silu(total[0]) * total[1]).astype(jnp.bfloat16)
    inner = lax.all_gather(inner, "dp", axis=0, tiled=True)
    term = jnp.dot(inner, down, preferred_element_type=jnp.float32)
    return (wide + lax.psum(term, "mp")).astype(jnp.bfloat16)


def wide_body(
    hidden_in, layer_gain, gate_proj, up_proj, down_proj, final_gain, teacher_rows, send_counts, doc_ids
):
    phases = lax.axis_size("section")
    count_data = lax.axis_size("dp")
    phase_pos = lax.axis_index("section")
    data_pos = lax.axis_index("dp")
    model_pos = lax.axis_index("mp")
    tokens, narrow = hidden_in.shape[1:]
    rows = lax.all_gather(hidden_in[0], "section", axis=0)
    rows = lax.all_gather(rows, "mp", axis=2, tiled=True)
    rows = lax.all_to_all(rows, "dp", split_axis=2, concat_axis=1, tiled=True)
    features = rows.shape[2]
    rows = rows.reshape(-1, features)
    ring = [(s, (s + 1) % phases) for s in range(phases)]
    for repeat in range(gate_proj.shape[0]):
        gain_row = lax.dynamic_slice_in_dim(layer_gain[repeat, 0], data_pos * features, features, 0)
        for phase in range(phases):
            fresh = wide_layer(
                rows, gain_row, gate_proj[repeat, 0], up_proj[repeat, 0], down_proj[repeat, 0]
            )
            rows = lax.ppermute(jnp.where(phase_pos == phase, fresh, rows), "section", ring)
    rows = lax.all_gather(rows, "section", axis=0)[0]
    rows = lax.dynamic_index_in_dim(
        rows.reshape(phases, count_data * tokens, features), phase_pos, 0, keepdims=False
    )
    rows = lax.all_to_all(rows, "dp", split_axis=0, concat_axis=1, tiled=True)
    final = lax.dynamic_slice_in_dim(rows, model_pos * narrow, narrow, 1)
    teacher = teacher_rows[0, 0].reshape(count_data, -1, narrow)
    capacity = teacher.shape[1]
    arrived = lax.all_to_all(teacher, "dp", split_axis=0, concat_axis=0, tiled=True)
    counts = lax.all_gather(send_counts[0, 0], "dp", axis=0)
    per_source = lax.dynamic_index_in_dim(counts, data_pos, 1, keepdims=False)
    end_rows = jnp.cumsum(per_source)
    starts = end_rows - per_source
    positions = jnp.arange(tokens, dtype=jnp.int32)
    source_of = jnp.sum((end_rows[None, :] <= positions[:, None]).astype(jnp.int32), axis=1)
    flat_index = source_of * capacity + positions - starts[source_of]
    targets = arrived.reshape(-1, narrow)[flat_index].astype(jnp.float32)
    return distil(
        final,
        targets,
        weights_of_rows(doc_ids[0, 0]),
        final_gain,
        lambda value: lax.psum(value, "mp"),
    )


def solution(mesh):
    in_specs = (
        P("section", "dp", "mp"),
        P(None, "section", None),
        P(None, "section", "dp", "mp"),
        P(None, "section", "dp", "mp"),
        P(None, "section", "mp", "dp"),
        P("mp"),
        P("section", "dp", None, "mp"),
        P("section", "dp", None),
        P("section", "dp", None),
    )
    out_specs = (P("section", "dp", "mp"), P("section", "dp"))
    sizes = tuple(mesh.shape[axis] for axis in AXES)
    body = fast_body if sizes == (2, 4, 4) else wide_body
    return jax.shard_map(body, mesh=mesh, in_specs=in_specs, out_specs=out_specs, check_vma=False)
```

```python
import functools

import jax
import jax.numpy as jnp
from jax import lax
from jax.experimental import pallas as pl
from jax.experimental.pallas import tpu as pltpu
from jax.sharding import PartitionSpec as P

D = 8192
DOCS = 8
EPSILON = 1e-05
AXES = ("section", "dp", "mp")
TILE = 512
COST = 1
VMEM_LIMIT = 40 * 1024 * 1024


def swap_section(value):
    return lax.ppermute(value, "section", [(0, 1), (1, 0)])


def transpose_mesh(value):
    pairs = [(d * 4 + m, m * 4 + d) for d in range(4) for m in range(4)]
    return lax.ppermute(value, ("dp", "mp"), pairs)


def swap_dp(value, e):
    return lax.ppermute(value, "dp", [(d, d ^ e) for d in range(4)])


def swap_mp(value, k):
    return lax.ppermute(value, "mp", [(m, m ^ k) for m in range(4)])


def exchange(value, axis):
    return lax.all_to_all(value, axis, split_axis=0, concat_axis=0, tiled=True)


def either(is_own, start_own, start_other):
    pl.when(is_own)(start_own)
    pl.when(jnp.logical_not(is_own))(start_other)


def wide_product_kernel(number, swapped, relative, x0, x1, x2, x3, gain_ref, own, received, keep_ref, send_ref, rows_ref, held, sems):
    step = pl.program_id(0)
    steps = pl.num_programs(0)
    is_own = lax.axis_index("section") == number
    own_place = lax.axis_index("dp")
    if relative:
        own_place = own_place ^ lax.axis_index("mp")
    count = x0.shape[0]

    def fetch(j, step):
        slot = 2 * lax.rem(step, 2) + j
        columns = pl.ds(pl.multiple_of((2 * step + j) * TILE, TILE), TILE)

        def copy(source):
            return lambda: pltpu.make_async_copy(source.at[:, columns], held.at[slot], sems.at[slot]).start()

        either(is_own, copy(own), copy(received))

    @pl.when(step == 0)
    def _():
        fetch(0, 0)
        fetch(1, 0)
        for k, ref in enumerate((x0, x1, x2, x3)):
            place = own_place ^ k
            if swapped:
                place = 2 * (place % 2) + place // 2
            piece = ref[...].astype(jnp.float32) * gain_ref[...]
            rows_ref[pl.ds(pl.multiple_of(place * count, count), count), :] = piece.astype(jnp.bfloat16)

    for j in range(2):

        @pl.when(step + 1 < steps)
        def _():
            fetch(j, step + 1)

        slot = 2 * lax.rem(step, 2) + j
        pltpu.make_async_copy(own.at[:, pl.ds(0, TILE)], held.at[slot], sems.at[slot]).wait()
        product = jnp.dot(rows_ref[...], held[slot], preferred_element_type=jnp.float32)
        keep_ref[:, j * TILE : (j + 1) * TILE] = product[: 2 * count]
        send_ref[:, j * TILE : (j + 1) * TILE] = product[2 * count :].astype(jnp.bfloat16)


def wide_product(number, swapped, rows, gain_row, own, received):
    groups = 4
    relative = isinstance(rows, list)
    count, depth = rows[0].shape
    width = own.shape[1]
    whole = lambda shape: pl.BlockSpec(shape, lambda t: (0,) * len(shape))
    if relative:
        piece_specs = [whole((count, depth))] * 4
    else:
        piece_specs = [pl.BlockSpec((None, count, depth), lambda t, k=k: (k, 0, 0)) for k in range(4)]
        rows = [rows] * 4
    return pl.pallas_call(
        functools.partial(wide_product_kernel, number, swapped, relative),
        grid=(width // (2 * TILE),),
        in_specs=piece_specs + [whole((1, depth))] + [pl.BlockSpec(memory_space=pl.ANY)] * 2,
        out_specs=[pl.BlockSpec((2 * count, 2 * TILE), lambda t: (0, t))] * 2,
        out_shape=[
            jax.ShapeDtypeStruct((2 * count, width), jnp.float32),
            jax.ShapeDtypeStruct((2 * count, width), jnp.bfloat16),
        ],
        scratch_shapes=[
            pltpu.VMEM((groups * count, depth), jnp.bfloat16),
            pltpu.VMEM((4, depth, TILE), jnp.bfloat16),
            pltpu.SemaphoreType.DMA((4,)),
        ],
        compiler_params=pltpu.CompilerParams(vmem_limit_bytes=VMEM_LIMIT),
        cost_estimate=pl.CostEstimate(
            flops=2 * groups * count * depth * width, bytes_accessed=2 * depth * width, transcendentals=0
        ),
        name="wide_product",
    )(*rows, gain_row, own, received)


def down_kernel(number, x0, x1, x2, x3a, x3b, own, received, out_ref, rows_ref, held, sems):
    step = pl.program_id(0)
    steps = pl.num_programs(0)
    is_own = lax.axis_index("section") == number
    data_pos = lax.axis_index("dp")
    groups = 4
    count, depth = x0.shape

    def fetch(tile):
        slot = lax.rem(tile, 2)
        columns = pl.ds(pl.multiple_of(tile * TILE, TILE), TILE)

        def copy(source):
            return lambda: pltpu.make_async_copy(source.at[:, columns], held.at[slot], sems.at[slot]).start()

        either(is_own, copy(own), copy(received))

    @pl.when(step == 0)
    def _():
        fetch(0)
        for e, piece in enumerate((x0, x1, x2)):
            rows_ref[pl.ds(pl.multiple_of((data_pos ^ e) * count, count), count), :] = piece[...]
        corner = pl.ds(pl.multiple_of((data_pos ^ 3) * count, count), count)
        rows_ref[corner, : depth // 2] = x3a[...]
        rows_ref[corner, depth // 2 :] = x3b[...]

    @pl.when(step + 1 < steps)
    def _():
        fetch(step + 1)

    slot = lax.rem(step, 2)
    pltpu.make_async_copy(own.at[:, pl.ds(0, TILE)], held.at[slot], sems.at[slot]).wait()
    product = jnp.dot(rows_ref[...], held[slot], preferred_element_type=jnp.float32)
    for g in range(groups):
        out_ref[g] = product[g * count : (g + 1) * count].astype(jnp.bfloat16)


def down_terms(number, pieces, own, received):
    groups = 4
    count, depth = pieces[0].shape
    features = own.shape[1]
    return pl.pallas_call(
        functools.partial(down_kernel, number),
        grid=(features // TILE,),
        in_specs=[pl.BlockSpec(piece.shape, lambda t: (0, 0)) for piece in pieces]
        + [pl.BlockSpec(memory_space=pl.ANY)] * 2,
        out_specs=pl.BlockSpec((groups, count, TILE), lambda t: (0, 0, t)),
        out_shape=jax.ShapeDtypeStruct((groups, count, features), jnp.bfloat16),
        scratch_shapes=[
            pltpu.VMEM((groups * count, depth), jnp.bfloat16),
            pltpu.VMEM((2, depth, TILE), jnp.bfloat16),
            pltpu.SemaphoreType.DMA((2,)),
        ],
        compiler_params=pltpu.CompilerParams(vmem_limit_bytes=VMEM_LIMIT),
        cost_estimate=pl.CostEstimate(
            flops=2 * groups * count * depth * features // COST,
            bytes_accessed=2 * depth * features // COST,
            transcendentals=0,
        ),
        name="down",
    )(*pieces, own, received)


def squares_by_place(rows):
    squares = jnp.stack([jnp.sum(jnp.square(rows[k].astype(jnp.float32)), axis=-1) for k in range(4)])
    own_place = lax.axis_index("dp")
    if isinstance(rows, list):
        own_place = own_place ^ lax.axis_index("mp")
    return [squares[i ^ own_place] for i in range(4)]


def tie(value, *earlier):
    return lax.optimization_barrier((value, earlier))[0]


def sum_squares(chunks, late):
    places = [jnp.stack(pieces) for pieces in zip(*[squares_by_place(rows) for rows in chunks])]
    keep, send = jnp.stack(places[0::2]), jnp.stack(places[1::2])
    got = swap_dp(send, 1)
    keep = keep + tie(got, late)
    return keep[0] + swap_dp(keep[1], 2)


def sum_first(partial, step):
    keep, send = partial
    count = keep.shape[0] // 2
    got = swap_dp(send, step)
    onward = (keep[count:] + got[count:].astype(jnp.float32)).astype(jnp.bfloat16)
    return keep[:count], got[:count], onward


def sum_second(state, step):
    keep, got, onward = state
    return keep + got.astype(jnp.float32) + swap_dp(onward, step).astype(jnp.float32)


def enter(own):
    return [own] + [swap_mp(own, k) for k in (1, 2, 3)]


def add_terms(own, terms):
    return (own.astype(jnp.float32) + jnp.sum(terms.astype(jnp.float32), axis=0)).astype(jnp.bfloat16)


def activate(states, squares):
    scale = lax.rsqrt(squares / D + EPSILON)[:, None]
    gate_rows, up_rows = sum_second(states[0], 2) * scale, sum_second(states[1], 1) * scale
    return (jax.nn.silu(gate_rows) * up_rows).astype(jnp.bfloat16)


def fast_final(hidden_in, layer_gain, gate, up, down, teacher, counts):
    tokens, features = hidden_in.shape[1:]
    half = gate.shape[1] // 2
    count = tokens // 2
    is_first = lax.axis_index("section") == 0
    gain = lax.dynamic_slice_in_dim(layer_gain[0, 0], lax.axis_index("dp") * features, features, 0)
    other_gain = swap_section(gain)
    received = [swap_section(tie(gate, other_gain))]
    owns = [transpose_mesh(hidden_in[0, i * count : (i + 1) * count]) for i in range(2)]
    received.append(swap_section(tie(up, owns[0])))
    targets = fast_targets(*tie((teacher, counts), owns[0]), tokens)
    for number in range(2):
        gain_row = jnp.where(is_first == (number == 0), gain, other_gain)[None, :]

        def products(which, pieces):
            return wide_product(
                number, which == 0, pieces, gain_row, (gate, up)[which], received[which]
            )

        if not number:
            rows = enter(owns[0])
            rows, owns[1], targets, later_down = lax.optimization_barrier((rows, owns[1], targets, down))
            received.append(swap_section(later_down))
            later_rows = enter(owns[1])
        first = products(0, rows)
        second = products(1, rows if number else tie(rows, first[0]))
        later_rows = tie(later_rows, second[0])
        states = [sum_first(first, 1), sum_first(second, 2)]
        later_first = products(0, later_rows)
        later_second = products(1, tie(later_rows, states[0][2]))
        later_states = [sum_first(later_first, 1), sum_first(later_second, 2)]
        squares, later_squares = sum_squares([rows, later_rows], later_second[0])
        inner, later_inner = activate(states, squares), activate(later_states, later_squares)
        along = [swap_dp(inner, 1), swap_dp(inner, 2)]
        later_along = [swap_dp(later_inner, 1), swap_dp(later_inner, 2)]
        corner = [swap_dp(along[1][:, :half], 1), swap_dp(along[0][:, half:], 2)]
        terms = exchange(down_terms(number, [inner] + along + corner, down, received[2]), "mp")
        corner = [swap_dp(later_along[1][:, :half], 1), swap_dp(later_along[0][:, half:], 2)]
        owns[0] = add_terms(owns[0], terms)
        if not number:
            rows = enter(owns[0])
        terms = down_terms(number, [later_inner] + later_along + corner, down, received[2])
        rows = tie(rows, terms)
        owns[1] = add_terms(owns[1], exchange(tie(terms, owns[0]), "mp"))
        if not number:
            later_rows = enter(owns[1])
    return jnp.concatenate([transpose_mesh(own) for own in owns], axis=0), targets


def fast_targets(teacher, counts, token_count):
    capacity = teacher.shape[0] // 4
    features = teacher.shape[1]
    arrived = lax.all_to_all(
        teacher.reshape(4, capacity, features), "dp", split_axis=0, concat_axis=0, tiled=True
    )
    all_counts = lax.all_to_all(
        counts.reshape(4, 1).astype(jnp.bfloat16), "dp", split_axis=0, concat_axis=0, tiled=True
    )
    per_source = all_counts[:, 0].astype(jnp.int32)
    end_rows = jnp.cumsum(per_source)
    starts = end_rows - per_source
    positions = jnp.arange(token_count, dtype=jnp.int32)
    source_of = jnp.sum((end_rows[None, :] <= positions[:, None]).astype(jnp.int32), axis=1)
    matching = source_of[:, None] == jnp.arange(4, dtype=jnp.int32)[None, :]
    first_row = jnp.sum(jnp.where(matching, starts[None, :], 0), axis=1)
    flat_index = source_of * capacity + positions - first_row
    return arrived.reshape(-1, features)[flat_index].astype(jnp.float32)


def weights_of_rows(doc_row):
    member = (doc_row[:, None] == jnp.arange(DOCS, dtype=jnp.int32)[None, :]).astype(jnp.float32)
    doc_sizes = jnp.sum(member, axis=0)
    return jnp.sum(member * (1.0 / doc_sizes)[None, :], axis=1)


def distil(final, targets, row_weight, final_gain, sum_features):
    wide = final.astype(jnp.float32)
    gain_row = final_gain[None, :]
    squares = sum_features(jnp.sum(wide * wide, axis=-1))
    rscale = lax.rsqrt(squares / D + EPSILON)
    normal_rows = wide * rscale[:, None]
    residual = normal_rows * gain_row - targets
    d_student = row_weight[:, None] * residual
    sums = sum_features(
        jnp.stack(
            [
                jnp.sum(normal_rows * gain_row * d_student, axis=-1),
                jnp.sum(residual * residual, axis=-1),
            ]
        )
    )
    d_hidden = rscale[:, None] * (gain_row * d_student - normal_rows * sums[0][:, None] / D)
    doc_loss = jnp.sum(row_weight * 0.5 * sums[1]) / (DOCS * D)
    return d_hidden[None], doc_loss.reshape(1, 1)


def distil_once(final, targets, row_weight, final_gain):
    wide = final.astype(jnp.float32)
    features = wide.shape[1]
    gained = wide * final_gain[None, :]
    squares = jnp.sum(wide * wide, axis=-1)
    rough = gained * lax.rsqrt(squares / features + EPSILON)[:, None] - targets
    local = jnp.stack(
        [squares, jnp.sum(rough * rough, axis=-1), jnp.sum(gained * rough, axis=-1), jnp.sum(gained * gained, axis=-1)]
    )
    squares, rough_squares, crossed, gained_squares = jnp.moveaxis(lax.all_gather(local, "mp"), 1, 0)
    rscale = lax.rsqrt(jnp.sum(squares, axis=0) / D + EPSILON)
    shift = rscale[None, :] - lax.rsqrt(squares / features + EPSILON)
    errors = jnp.sum(rough_squares + shift * (2.0 * crossed + shift * gained_squares), axis=0)
    inner_sum = row_weight * rscale * jnp.sum(crossed + shift * gained_squares, axis=0)
    gain_row = final_gain[None, :]
    normal_rows = wide * rscale[:, None]
    d_student = row_weight[:, None] * (normal_rows * gain_row - targets)
    d_hidden = rscale[:, None] * (gain_row * d_student - normal_rows * inner_sum[:, None] / D)
    doc_loss = jnp.sum(row_weight * 0.5 * errors) / (DOCS * D)
    return d_hidden[None], doc_loss.reshape(1, 1)


def fast_body(
    hidden_in, layer_gain, gate_proj, up_proj, down_proj, final_gain, teacher_rows, send_counts, doc_ids
):
    final, targets = fast_final(
        hidden_in,
        layer_gain,
        gate_proj[0, 0],
        up_proj[0, 0],
        down_proj[0, 0],
        teacher_rows[0, 0],
        send_counts[0, 0],
    )
    return distil_once(final, targets, weights_of_rows(doc_ids[0, 0]), final_gain)


def wide_layer(rows, gain_row, gate, up, down):
    wide = rows.astype(jnp.float32)
    squares = lax.psum(jnp.sum(wide * wide, axis=-1, keepdims=True), "dp")
    scale = lax.rsqrt(squares / D + EPSILON)
    normed = (wide * scale * gain_row[None, :]).astype(jnp.bfloat16)
    both = jnp.stack(
        [jnp.dot(normed, weight, preferred_element_type=jnp.float32) for weight in (gate, up)]
    )
    total = lax.psum_scatter(both, "dp", scatter_dimension=1, tiled=True)
    inner = (jax.nn.silu(total[0]) * total[1]).astype(jnp.bfloat16)
    inner = lax.all_gather(inner, "dp", axis=0, tiled=True)
    term = jnp.dot(inner, down, preferred_element_type=jnp.float32)
    return (wide + lax.psum(term, "mp")).astype(jnp.bfloat16)


def wide_body(
    hidden_in, layer_gain, gate_proj, up_proj, down_proj, final_gain, teacher_rows, send_counts, doc_ids
):
    phases = lax.axis_size("section")
    count_data = lax.axis_size("dp")
    phase_pos = lax.axis_index("section")
    data_pos = lax.axis_index("dp")
    model_pos = lax.axis_index("mp")
    tokens, narrow = hidden_in.shape[1:]
    rows = lax.all_gather(hidden_in[0], "section", axis=0)
    rows = lax.all_gather(rows, "mp", axis=2, tiled=True)
    rows = lax.all_to_all(rows, "dp", split_axis=2, concat_axis=1, tiled=True)
    features = rows.shape[2]
    rows = rows.reshape(-1, features)
    ring = [(s, (s + 1) % phases) for s in range(phases)]
    for repeat in range(gate_proj.shape[0]):
        gain_row = lax.dynamic_slice_in_dim(layer_gain[repeat, 0], data_pos * features, features, 0)
        for phase in range(phases):
            fresh = wide_layer(
                rows, gain_row, gate_proj[repeat, 0], up_proj[repeat, 0], down_proj[repeat, 0]
            )
            rows = lax.ppermute(jnp.where(phase_pos == phase, fresh, rows), "section", ring)
    rows = lax.all_gather(rows, "section", axis=0)[0]
    rows = lax.dynamic_index_in_dim(
        rows.reshape(phases, count_data * tokens, features), phase_pos, 0, keepdims=False
    )
    rows = lax.all_to_all(rows, "dp", split_axis=0, concat_axis=1, tiled=True)
    final = lax.dynamic_slice_in_dim(rows, model_pos * narrow, narrow, 1)
    teacher = teacher_rows[0, 0].reshape(count_data, -1, narrow)
    capacity = teacher.shape[1]
    arrived = lax.all_to_all(teacher, "dp", split_axis=0, concat_axis=0, tiled=True)
    counts = lax.all_gather(send_counts[0, 0], "dp", axis=0)
    per_source = lax.dynamic_index_in_dim(counts, data_pos, 1, keepdims=False)
    end_rows = jnp.cumsum(per_source)
    starts = end_rows - per_source
    positions = jnp.arange(tokens, dtype=jnp.int32)
    source_of = jnp.sum((end_rows[None, :] <= positions[:, None]).astype(jnp.int32), axis=1)
    flat_index = source_of * capacity + positions - starts[source_of]
    targets = arrived.reshape(-1, narrow)[flat_index].astype(jnp.float32)
    return distil(
        final,
        targets,
        weights_of_rows(doc_ids[0, 0]),
        final_gain,
        lambda value: lax.psum(value, "mp"),
    )


def solution(mesh):
    in_specs = (
        P("section", "dp", "mp"),
        P(None, "section", None),
        P(None, "section", "dp", "mp"),
        P(None, "section", "dp", "mp"),
        P(None, "section", "mp", "dp"),
        P("mp"),
        P("section", "dp", None, "mp"),
        P("section", "dp", None),
        P("section", "dp", None),
    )
    out_specs = (P("section", "dp", "mp"), P("section", "dp"))
    sizes = tuple(mesh.shape[axis] for axis in AXES)
    body = fast_body if sizes == (2, 4, 4) else wide_body
    return jax.shard_map(body, mesh=mesh, in_specs=in_specs, out_specs=out_specs, check_vma=False)
```
